128 devices in a mesh: dp: 8 (over x, core), tensor: 16 (over z, y).
Axes of the slice: x: 4, y: 4, z: 4, core: 2. Of those that a mesh axis runs over, the one named last changes fastest.
Arguments:
- hidden_acts: bfloat16 [16384, 14336], P('dp', 'tensor'), may hold values from -6 to 6
- cotangent: bfloat16 [16384, 4096], P(('dp', 'tensor')), may hold values from -0.125 to 0.125
- error_buffer: bfloat16 [8, 4096, 14336], P('dp', None, 'tensor'), may hold values from -6 to 6
- q_start: float32 [14336, 32], P('tensor'), may hold values from -0.046875 to 0.046875
Outputs:
- new_error: bfloat16 [8, 4096, 14336], P('dp', None, 'tensor')
- q_mean: float32 [14336, 32], P('tensor')
The draws below stay inside these ranges and needn't reach their ends.
All inputs are finite; a program needn't handle non-finite values.
Results may differ from the reference program's by a relative error of at most 0.00045.
Values may be sent and summed in bfloat16 or wider, within the bound.
No kernel may reach another device: no remote copies, remote signals or barrier semaphores. Data moves between devices by JAX's collectives and lax.ppermute only.
A program may use at most 128 MiB of HBM per device.

```python
import jax
import jax.numpy as jnp
from jax import lax

D = 4096
FF = 14336
RANK = 32
TOK_DEV = 2048
TOKENS = 16384
REPLICAS = 8
N_DP = 8


def shard_levels(rng, shape, pieces, low, top_value):
    def one(position, blocks):
        steps = jax.random.uniform(jax.random.fold_in(jax.random.fold_in(rng, 6), position), (blocks,), jnp.float32, low / len(pieces), top_value / len(pieces))
        return jnp.repeat(jnp.exp(steps), shape[position] // blocks).reshape((-1,) + (1,) * (len(shape) - position - 1))

    factor_of = one(*pieces[0])
    for cut in pieces[1:]:
        factor_of = factor_of * one(*cut)
    return factor_of


def normal_values(key, dims, scale, bound, shards=(), held_as=jnp.bfloat16):
    factor_of = shard_levels(key, dims, shards, -0.22, 0.18) if shards else 1.0
    entries = jax.random.normal(key, dims, jnp.float32) * scale * factor_of
    return jnp.minimum(jnp.maximum(entries, -bound), bound).astype(held_as)


def setup_inputs(seed: int = 0) -> dict:
    key_of = jax.random.split(jax.random.key(seed), 5)
    hidden_acts = normal_values(key_of[0], (TOKENS, FF), 1.0, 6.0, ((0, 8), (1, 16)))
    cotangent = normal_values(key_of[1], (TOKENS, D), (TOK_DEV ** -0.5), 0.125, ((0, 128),))
    error_buffer = normal_values(key_of[2], (REPLICAS, D, FF), 1.0, 6.0, ((0, 8), (2, 16)))
    q_start = normal_values(key_of[3], (FF, RANK), FF ** -0.5, 0.046875, ((0, 16),), jnp.float32)
    return {"hidden_acts": hidden_acts, "cotangent": cotangent, "error_buffer": error_buffer, "q_start": q_start}


def reference(hidden_acts, cotangent, error_buffer, q_start):
    highest = lax.Precision.HIGHEST
    merged_list = []
    for replica in range(N_DP):
        g_rows = cotangent[replica * TOK_DEV:(replica + 1) * TOK_DEV]
        h_rows = hidden_acts[replica * TOK_DEV:(replica + 1) * TOK_DEV]
        grad_part = jnp.dot(g_rows.T.astype(jnp.float32), h_rows.astype(jnp.float32), preferred_element_type=jnp.float32)
        merged_list.append(grad_part + error_buffer[replica].astype(jnp.float32))
    power = jnp.zeros((D, RANK), jnp.float32)
    for merged in merged_list:
        power = power + jnp.dot(merged, q_start, precision=highest)
    gram_matrix = jnp.dot(power.T, power, precision=highest)
    factor_lower = jnp.linalg.cholesky(gram_matrix)
    basis = jax.scipy.linalg.solve_triangular(factor_lower, power.T, lower=True).T
    q_total = jnp.zeros((FF, RANK), jnp.float32)
    for merged in merged_list:
        q_total = q_total + jnp.dot(merged.T, basis, precision=highest)
    q_mean = q_total / N_DP
    update = jnp.dot(basis, q_mean.T, precision=highest)
    new_error = jnp.stack([(merged - update).astype(jnp.bfloat16) for merged in merged_list])
    return (new_error, q_mean)
```

```python
import jax
import jax.numpy as jnp
from jax import lax
from jax.experimental import pallas as pl
from jax.experimental.pallas import tpu as pltpu
from jax.sharding import PartitionSpec as P

AXES = ("dp", "tensor")
RANK = 32
NX, NC, NZ, NY = 4, 2, 4, 4
N_DP = NX * NC
TOK = 128
TILE = 128
BLOCK = 512
F32, BF16 = jnp.float32, jnp.bfloat16
SMEM = pl.BlockSpec(memory_space=pltpu.SMEM)


def receive_from(x=0, c=0, z=0, y=0):
    pairs = []
    for ix in range(NX):
        for ic in range(NC):
            for iz in range(NZ):
                for iy in range(NY):
                    target = ((ix * NC + ic) * NZ + iz) * NY + iy
                    source = (((ix + x) % NX * NC + (ic + c) % NC) * NZ + (iz + z) % NZ) * NY + (iy + y) % NY
                    pairs.append((source, target))
    return pairs


def fetch(array, **offsets):
    return lax.ppermute(array, AXES, receive_from(**offsets))


def around(arrays, axis):
    return [arrays[0]] + [fetch(arrays[k], **{axis: k}) for k in (1, 2, 3)]


def f32(*shape):
    return jax.ShapeDtypeStruct(shape, F32)


def bf16(*shape):
    return jax.ShapeDtypeStruct(shape, BF16)


def whole(array):
    zeros = (0,) * len(array.shape)
    return pl.BlockSpec(tuple(array.shape), lambda *_: zeros)


def kernel_call(body, grid, operands, in_specs, outs, out_specs, scratch=(), aliases=None, vmem_mib=24, after=()):
    count = len(operands)
    operands = [*operands, *after]
    in_specs = [*in_specs, *[pl.BlockSpec(memory_space=pltpu.HBM)] * len(after)]

    def call(*refs):
        body(*refs[:count], *refs[count + len(after):])

    return pl.pallas_call(
        call,
        grid=(grid,),
        in_specs=[whole(a) if s is None else s for a, s in zip(operands, in_specs)],
        out_specs=[whole(a) if s is None else s for a, s in zip(outs, out_specs)],
        out_shape=outs,
        scratch_shapes=list(scratch),
        input_output_aliases=aliases or {},
        compiler_params=pltpu.CompilerParams(vmem_limit_bytes=vmem_mib * 2 ** 20),
        cost_estimate=pl.CostEstimate(flops=2 ** 20, bytes_accessed=2 ** 16, transcendentals=0),
    )(*operands)


def split3(value):
    high = value.astype(BF16)
    rest = value - high.astype(F32)
    middle = rest.astype(BF16)
    low = (rest - middle.astype(F32)).astype(BF16)
    return jnp.concatenate([high, middle, low], axis=0)


def fold3(product):
    return product[:RANK] + (product[RANK:2 * RANK] + product[2 * RANK:])


def dot_nt(a, b):
    return lax.dot_general(a, b, (((1,), (1,)), ((), ())), preferred_element_type=F32)


def dot_nn(a, b):
    return jnp.dot(a, b, preferred_element_type=F32)


def hq_body(q_t, h, out, pieces):
    @pl.when(pl.program_id(0) == 0)
    def _():
        pieces[...] = split3(q_t[...])

    part = fold3(dot_nt(pieces[...], h[...]))
    for y in range(NY):
        out[y] = part[:, y * TOK:(y + 1) * TOK]


def eq_body(q_t, e, out, pieces):
    @pl.when(pl.program_id(0) == 0)
    def _():
        pieces[...] = split3(q_t[...])

    out[...] = fold3(dot_nt(pieces[...], e[...]))


def power_body(hq, ct, eq, out, lhs):
    @pl.when(pl.program_id(0) == 0)
    def _():
        total = hq[0]
        for t in range(1, NZ * NY):
            total += hq[t]
        lhs[...] = split3(total)

    term = fold3(dot_nt(lhs[...], ct[...])) + eq[...]
    for j in range(BLOCK // TILE):
        for i in range(RANK // 8):
            out[j * (RANK // 8) + i] = term[i * 8:(i + 1) * 8, j * TILE:(j + 1) * TILE]


def tile_sum_body(tiles, out):
    totals = [tiles[k] for k in range(4)]
    for k in range(4, tiles.shape[0]):
        totals[k % 4] += tiles[k]
    out[...] = jnp.broadcast_to(((totals[0] + totals[1]) + (totals[2] + totals[3]))[None], out.shape)


def cp_body(tiles, ct, power, pieces, out, acc):
    i = pl.program_id(0)

    @pl.when(i == 0)
    def _():
        acc[...] = jnp.zeros_like(acc)

    n = RANK // 8
    block = jnp.concatenate([
        jnp.concatenate([tiles[j * n + k] for k in range(n)], axis=0) for j in range(BLOCK // TILE)
    ], axis=1)
    power[...] = block
    split = split3(block)
    pieces[...] = split
    acc[...] += fold3(dot_nn(split, ct[...]))

    @pl.when(i == pl.num_programs(0) - 1)
    def _():
        out[...] = jnp.broadcast_to(acc[...][None], out.shape)


def basis_body(power, pieces, e, ep, inverse, basis, acc, gram):
    i = pl.program_id(0)

    @pl.when(i == 0)
    def _():
        acc[...] = jnp.zeros_like(acc)
        gram[...] = lax.dot_general(
            power[...], power[...], (((1,), (1,)), ((), ())), precision=lax.Precision.HIGHEST, preferred_element_type=F32
        )

    acc[...] += fold3(dot_nn(pieces[...], e[...]))

    @pl.when(i == pl.num_programs(0) - 1)
    def _():
        ep[...] = acc[...]
        row = lax.broadcasted_iota(jnp.int32, (RANK, 2 * RANK), 0)
        column = lax.broadcasted_iota(jnp.int32, (RANK, 2 * RANK), 1)
        work = jnp.concatenate([gram[...], jnp.zeros((RANK, RANK), F32)], axis=1)
        work = jnp.where(column == row + RANK, 1.0, work)
        for j in range(RANK):
            factor = work[:, j:j + 1] / work[j:j + 1, j:j + 1]
            work = work - jnp.where(row > j, factor, 0.0) * work[j:j + 1, :]
        pivots = jnp.sum(jnp.where(column == row, work, 0.0), axis=1, keepdims=True)
        inv = work[:, RANK:] / jnp.sqrt(pivots)
        inverse[...] = inv
        b = jnp.dot(inv, power[...], precision=lax.Precision.HIGHEST, preferred_element_type=F32)
        b = split3(b)
        high, middle, low = b[:RANK], b[RANK:2 * RANK], b[2 * RANK:]
        basis[...] = jnp.concatenate([high, high, middle, high, low, middle], axis=0)


def q_body(cp, h, ep, out, acc):
    i = pl.program_id(0)

    @pl.when(i == 0)
    def _():
        acc[...] = ep[...]

    left = split3(jnp.concatenate([cp[y] for y in range(NY)], axis=1))
    acc[...] += fold3(dot_nn(left, h[...]))

    @pl.when(i == NZ - 1)
    def _():
        out[...] = acc[...]


def mean_body(inverse, p0, p1, p2, p3, q_mean, pieces):
    total = (p0[...] + p1[...]) + (p2[...] + p3[...])
    mean = jnp.dot(inverse[...], total, precision=lax.Precision.HIGHEST, preferred_element_type=F32) * (1.0 / N_DP)
    q_mean[...] = mean
    s = split3(mean)
    high, middle, low = s[:RANK], s[RANK:2 * RANK], s[2 * RANK:]
    pieces[...] = jnp.concatenate([high, middle, high, low, high, middle], axis=0)


def error_body(g, h, basis, q, e, out):
    left = jnp.concatenate([g[t] for t in range(NZ * NY)], axis=1)
    acc = dot_nn(left, h[...])
    update = lax.dot_general(basis[...], q[...], (((0,), (0,)), ((), ())), preferred_element_type=F32)
    out[...] = ((acc + e[...].astype(F32)) - update).astype(BF16)


def error_call(gathered, h, basis, q, e):
    rows, columns = e.shape
    in_rows = pl.BlockSpec((BLOCK, columns), lambda i: (i, 0))
    return kernel_call(
        error_body, rows // BLOCK, [gathered, h, basis, q, e],
        [pl.BlockSpec((NZ * NY, BLOCK, TOK), lambda i: (0, i, 0)), None,
         pl.BlockSpec((basis.shape[0], BLOCK), lambda i: (0, i)), None, in_rows],
        [bf16(rows, columns)], [in_rows], vmem_mib=40,
    )[0]


def on_device(hidden, cotangent, error, q_start):
    error = error[0]
    rows = cotangent.shape[1]
    columns = hidden.shape[1]
    n_blocks = rows // BLOCK

    ct = cotangent.T
    gathered = lax.all_gather(ct, "tensor", axis=0)

    q_t = q_start.T
    (hq,) = kernel_call(
        hq_body, NZ, [q_t, hidden], [None, pl.BlockSpec((4 * TOK, columns), lambda i: (i, 0))],
        [f32(NZ * NY, RANK, TOK)], [pl.BlockSpec((NY, RANK, TOK), lambda i: (i, 0, 0))],
        scratch=[pltpu.VMEM((3 * RANK, columns), BF16)],
    )
    hq = lax.all_to_all(hq, "tensor", 0, 0)
    row_spec = pl.BlockSpec((BLOCK, columns), lambda i: (i, 0))
    column_spec = pl.BlockSpec((RANK, BLOCK), lambda i: (0, i))
    (eq,) = kernel_call(
        eq_body, n_blocks, [q_t, error], [None, row_spec], [f32(RANK, rows)], [column_spec],
        scratch=[pltpu.VMEM((3 * RANK, columns), BF16)],
    )
    stack_specs = [
        pl.BlockSpec((BLOCK, 4 * TOK), lambda i, n=n: (jnp.clip(i - 2 * n, 0, 1), 0)) for n in range(4)
    ]
    ct_spec = pl.BlockSpec((BLOCK, TOK), lambda i: (i, 0))
    n_tiles = RANK // 8 * (rows // TILE)
    tile_spec = pl.BlockSpec((n_tiles // n_blocks, 8, TILE), lambda i: (i, 0, 0))
    (tiles,) = kernel_call(
        power_body, n_blocks, [hq, ct, eq], [None, ct_spec, column_spec], [f32(n_tiles, 8, TILE)], [tile_spec],
        scratch=[pltpu.VMEM((3 * RANK, TOK), BF16)],
    )
    tiles = lax.all_to_all(tiles, AXES, 0, 0)
    (tiles,) = kernel_call(tile_sum_body, 1, [tiles], [None], [f32(n_tiles, 8, TILE)], [None])
    tiles = lax.all_to_all(tiles, AXES, 0, 0)
    power, pieces, cp = kernel_call(
        cp_body, n_blocks, [tiles, ct], [tile_spec, ct_spec],
        [f32(RANK, rows), bf16(3 * RANK, rows), f32(NZ * NY, RANK, TOK)],
        [column_spec, pl.BlockSpec((3 * RANK, BLOCK), lambda i: (0, i)), None],
        scratch=[pltpu.VMEM((RANK, TOK), F32)],
    )
    cp = lax.all_to_all(cp, "tensor", 0, 0)
    ep, inverse, basis = kernel_call(
        basis_body, n_blocks, [power, pieces, error],
        [None, pl.BlockSpec((3 * RANK, BLOCK), lambda i: (0, i)), row_spec],
        [f32(RANK, columns), f32(RANK, RANK), bf16(6 * RANK, rows)], [None] * 3,
        scratch=[pltpu.VMEM((RANK, columns), F32), pltpu.VMEM((RANK, RANK), F32)],
    )
    (q_raw,) = kernel_call(
        q_body, NZ, [cp, hidden, ep],
        [pl.BlockSpec((NY, RANK, TOK), lambda i: (i, 0, 0)), pl.BlockSpec((4 * TOK, columns), lambda i: (i, 0)), None],
        [f32(RANK, columns)], [None], scratch=[pltpu.VMEM((RANK, columns), F32)],
    )
    q_raw = q_raw + fetch(q_raw, c=1)
    q_mean, q_pieces = kernel_call(
        mean_body, 1, [inverse, *around([q_raw] * 4, "x")], [None] * 5,
        [f32(RANK, columns), bf16(6 * RANK, columns)], [None] * 2,
    )

    out = error_call(gathered, hidden, basis, q_pieces, error)
    return out[None], q_mean.T


def solution(mesh):
    placed = (
        P("dp", "tensor"),
        P(("dp", "tensor"), None),
        P("dp", None, "tensor"),
        P("tensor", None),
    )
    return jax.shard_map(
        on_device,
        mesh=mesh,
        in_specs=placed,
        out_specs=(P("dp", None, "tensor"), P("tensor", None)),
        check_vma=False,
    )
```

```python
import jax
import jax.numpy as jnp
from jax import lax
from jax.experimental import pallas as pl
from jax.experimental.pallas import tpu as pltpu
from jax.sharding import PartitionSpec as P

AXES = ("dp", "tensor")
RANK = 32
NX, NC, NZ, NY = 4, 2, 4, 4
N_DP = NX * NC
TOK = 128
BLOCK = 512
F32, BF16 = jnp.float32, jnp.bfloat16
SMEM = pl.BlockSpec(memory_space=pltpu.SMEM)


def receive_from(x=0, c=0, z=0, y=0):
    pairs = []
    for ix in range(NX):
        for ic in range(NC):
            for iz in range(NZ):
                for iy in range(NY):
                    target = ((ix * NC + ic) * NZ + iz) * NY + iy
                    source = (((ix + x) % NX * NC + (ic + c) % NC) * NZ + (iz + z) % NZ) * NY + (iy + y) % NY
                    pairs.append((source, target))
    return pairs


def fetch(array, **offsets):
    return lax.ppermute(array, AXES, receive_from(**offsets))


def around(arrays, axis):
    return [arrays[0]] + [fetch(arrays[k], **{axis: k}) for k in (1, 2, 3)]


def f32(*shape):
    return jax.ShapeDtypeStruct(shape, F32)


def bf16(*shape):
    return jax.ShapeDtypeStruct(shape, BF16)


def whole(array):
    zeros = (0,) * len(array.shape)
    return pl.BlockSpec(tuple(array.shape), lambda *_: zeros)


def kernel_call(body, grid, operands, in_specs, outs, out_specs, scratch=(), aliases=None, vmem_mib=16, after=()):
    count = len(operands)
    operands = [*operands, *after]
    in_specs = [*in_specs, *[pl.BlockSpec(memory_space=pltpu.HBM)] * len(after)]

    def call(*refs):
        body(*refs[:count], *refs[count + len(after):])

    return pl.pallas_call(
        call,
        grid=(grid,),
        in_specs=[whole(a) if s is None else s for a, s in zip(operands, in_specs)],
        out_specs=[whole(a) if s is None else s for a, s in zip(outs, out_specs)],
        out_shape=outs,
        scratch_shapes=list(scratch),
        input_output_aliases=aliases or {},
        compiler_params=pltpu.CompilerParams(vmem_limit_bytes=vmem_mib * 2 ** 20),
        cost_estimate=pl.CostEstimate(flops=2 ** 20, bytes_accessed=2 ** 16, transcendentals=0),
    )(*operands)


def split3(value):
    high = value.astype(BF16)
    rest = value - high.astype(F32)
    middle = rest.astype(BF16)
    low = (rest - middle.astype(F32)).astype(BF16)
    return jnp.concatenate([high, middle, low], axis=0)


def fold3(product):
    return product[:RANK] + (product[RANK:2 * RANK] + product[2 * RANK:])


def dot_nt(a, b):
    return lax.dot_general(a, b, (((1,), (1,)), ((), ())), preferred_element_type=F32)


def dot_nn(a, b):
    return jnp.dot(a, b, preferred_element_type=F32)


def hq_body(q_t, h, out, pieces):
    @pl.when(pl.program_id(0) == 0)
    def _():
        pieces[...] = split3(q_t[...])

    part = fold3(dot_nt(pieces[...], h[...]))
    for y in range(NY):
        out[y] = part[:, y * TOK:(y + 1) * TOK]


def eq_body(q_t, e, out, pieces):
    @pl.when(pl.program_id(0) == 0)
    def _():
        pieces[...] = split3(q_t[...])

    out[...] = fold3(dot_nt(pieces[...], e[...]))


def power_body(hq, c, eq, out, lhs):
    @pl.when(pl.program_id(0) == 0)
    def _():
        total = hq[0]
        for t in range(1, NZ * NY):
            total += hq[t]
        lhs[...] = split3(total)

    term = fold3(dot_nn(lhs[...], c[...])) + eq[...]
    for j in range(out.shape[0]):
        out[j] = term[:, j * BLOCK:(j + 1) * BLOCK]


def sum_body(*refs):
    total = refs[0][...]
    for ref in refs[1:-1]:
        total += ref[...]
    refs[-1][...] = total


def sum_copies_body(*refs):
    total = (refs[0][...] + refs[1][...]) + (refs[2][...] + refs[3][...])
    refs[4][...] = jnp.broadcast_to(total[None], refs[4].shape)


def sum_pieces_body(pieces, out):
    total = pieces[0]
    for r in range(1, N_DP):
        total += pieces[r]
    out[...] = total


def cp_body(power_pieces, c, power, pieces, out, acc):
    i = pl.program_id(0)

    @pl.when(i == 0)
    def _():
        acc[...] = jnp.zeros_like(acc)

    block = jnp.concatenate([power_pieces[j] for j in range(power_pieces.shape[0])], axis=1)
    power[...] = block
    split = split3(block)
    pieces[...] = split
    acc[...] += fold3(dot_nt(split, c[...]))

    @pl.when(i == pl.num_programs(0) - 1)
    def _():
        out[...] = jnp.broadcast_to(acc[...][None], out.shape)


def basis_body(power, pieces, e, ep, inverse, basis, acc, gram):
    i = pl.program_id(0)

    @pl.when(i == 0)
    def _():
        acc[...] = jnp.zeros_like(acc)
        gram[...] = lax.dot_general(
            power[...], power[...], (((1,), (1,)), ((), ())), precision=lax.Precision.HIGHEST, preferred_element_type=F32
        )

    acc[...] += fold3(dot_nn(pieces[...], e[...]))

    @pl.when(i == pl.num_programs(0) - 1)
    def _():
        ep[...] = acc[...]
        row = lax.broadcasted_iota(jnp.int32, (RANK, 2 * RANK), 0)
        column = lax.broadcasted_iota(jnp.int32, (RANK, 2 * RANK), 1)
        work = jnp.concatenate([gram[...], jnp.zeros((RANK, RANK), F32)], axis=1)
        work = jnp.where(column == row + RANK, 1.0, work)
        for j in range(RANK):
            factor = work[:, j:j + 1] / work[j:j + 1, j:j + 1]
            work = work - jnp.where(row > j, factor, 0.0) * work[j:j + 1, :]
        pivots = jnp.sum(jnp.where(column == row, work, 0.0), axis=1, keepdims=True)
        inv = work[:, RANK:] / jnp.sqrt(pivots)
        inverse[...] = inv
        b = jnp.dot(inv, power[...], precision=lax.Precision.HIGHEST, preferred_element_type=F32)
        b = split3(b)
        high, middle, low = b[:RANK], b[RANK:2 * RANK], b[2 * RANK:]
        basis[...] = jnp.concatenate([high, high, middle, high, low, middle], axis=0)


def q_body(cp, h, ep, out, acc):
    i = pl.program_id(0)

    @pl.when(i == 0)
    def _():
        acc[...] = ep[...]

    left = split3(jnp.concatenate([cp[y] for y in range(NY)], axis=1))
    acc[...] += fold3(dot_nn(left, h[...]))

    @pl.when(i == NZ - 1)
    def _():
        out[...] = acc[...]


def mean_body(inverse, p0, p1, p2, p3, q_mean, pieces):
    total = (p0[...] + p1[...]) + (p2[...] + p3[...])
    mean = jnp.dot(inverse[...], total, precision=lax.Precision.HIGHEST, preferred_element_type=F32) * (1.0 / N_DP)
    q_mean[...] = mean
    s = split3(mean)
    high, middle, low = s[:RANK], s[RANK:2 * RANK], s[2 * RANK:]
    pieces[...] = jnp.concatenate([high, middle, high, low, high, middle], axis=0)


def rest_body(basis, q, e, out):
    update = lax.dot_general(basis[...], q[...], (((0,), (0,)), ((), ())), preferred_element_type=F32)
    out[...] = e[...].astype(F32) - update


def error_body(c, h, rest, out):
    gradient = lax.dot_general(c[...], h[...], (((0,), (0,)), ((), ())), preferred_element_type=F32)
    out[...] = (gradient + rest[...]).astype(BF16)


def error_calls(gathered, h, basis, q, e):
    rows, columns = e.shape
    wide = 2 * BLOCK
    in_rows = pl.BlockSpec((wide, columns), lambda i: (i, 0))
    (rest,) = kernel_call(
        rest_body, rows // wide, [basis, q, e],
        [pl.BlockSpec((basis.shape[0], wide), lambda i: (0, i)), None, in_rows], [f32(rows, columns)], [in_rows], vmem_mib=56,
    )
    in_rows = pl.BlockSpec((BLOCK, columns), lambda i: (i, 0))
    return kernel_call(
        error_body, rows // BLOCK, [gathered, h, rest],
        [pl.BlockSpec((gathered.shape[0], BLOCK), lambda i: (0, i)), None, in_rows],
        [bf16(rows, columns)], [in_rows], vmem_mib=56,
    )[0]


def on_device(hidden, cotangent, error, q_start):
    error = error[0]
    rows = cotangent.shape[1]
    columns = hidden.shape[1]
    n_blocks = rows // BLOCK

    gathered = lax.all_gather(cotangent, "tensor", axis=0, tiled=True)

    q_t = q_start.T
    (hq,) = kernel_call(
        hq_body, NZ, [q_t, hidden], [None, pl.BlockSpec((4 * TOK, columns), lambda i: (i, 0))],
        [f32(NZ * NY, RANK, TOK)], [pl.BlockSpec((NY, RANK, TOK), lambda i: (i, 0, 0))],
        scratch=[pltpu.VMEM((3 * RANK, columns), BF16)],
    )
    hq = lax.all_to_all(hq, "tensor", 0, 0)
    row_spec = pl.BlockSpec((BLOCK, columns), lambda i: (i, 0))
    column_spec = pl.BlockSpec((RANK, BLOCK), lambda i: (0, i))
    (eq,) = kernel_call(
        eq_body, n_blocks, [q_t, error], [None, row_spec], [f32(RANK, rows)], [column_spec],
        scratch=[pltpu.VMEM((3 * RANK, columns), BF16)],
    )
    stack_specs = [
        pl.BlockSpec((BLOCK, 4 * TOK), lambda i, n=n: (jnp.clip(i - 2 * n, 0, 1), 0)) for n in range(4)
    ]
    wide = n_blocks // 2
    c_spec = pl.BlockSpec((TOK, wide * BLOCK), lambda i: (0, i))
    wide_spec = pl.BlockSpec((RANK, wide * BLOCK), lambda i: (0, i))
    piece_spec = pl.BlockSpec((wide, RANK, BLOCK), lambda i: (i, 0, 0))
    (terms,) = kernel_call(
        power_body, 2, [hq, cotangent, eq], [None, c_spec, wide_spec], [f32(N_DP, RANK, BLOCK)], [piece_spec],
        scratch=[pltpu.VMEM((3 * RANK, TOK), BF16)],
    )
    terms = lax.all_to_all(terms, "dp", 0, 0)
    (piece,) = kernel_call(sum_pieces_body, 1, [terms], [None], [f32(RANK, BLOCK)], [None])
    (piece,) = kernel_call(sum_body, 1, around([piece] * 4, "y"), [None] * 4, [f32(RANK, BLOCK)], [None])
    (copies,) = kernel_call(
        sum_copies_body, 1, around([piece] * 4, "z"), [None] * 4, [f32(N_DP, RANK, BLOCK)], [None],
    )
    power_pieces = lax.all_to_all(copies, "dp", 0, 0)
    power, pieces, cp = kernel_call(
        cp_body, 2, [power_pieces, cotangent], [piece_spec, c_spec],
        [f32(RANK, rows), bf16(3 * RANK, rows), f32(NZ * NY, RANK, TOK)],
        [wide_spec, pl.BlockSpec((3 * RANK, wide * BLOCK), lambda i: (0, i)), None],
        scratch=[pltpu.VMEM((RANK, TOK), F32)],
    )
    cp = lax.all_to_all(cp, "tensor", 0, 0)
    ep, inverse, basis = kernel_call(
        basis_body, n_blocks, [power, pieces, error],
        [None, pl.BlockSpec((3 * RANK, BLOCK), lambda i: (0, i)), row_spec],
        [f32(RANK, columns), f32(RANK, RANK), bf16(6 * RANK, rows)], [None] * 3,
        scratch=[pltpu.VMEM((RANK, columns), F32), pltpu.VMEM((RANK, RANK), F32)],
    )
    (q_raw,) = kernel_call(
        q_body, NZ, [cp, hidden, ep],
        [pl.BlockSpec((NY, RANK, TOK), lambda i: (i, 0, 0)), pl.BlockSpec((4 * TOK, columns), lambda i: (i, 0)), None],
        [f32(RANK, columns)], [None], scratch=[pltpu.VMEM((RANK, columns), F32)],
    )
    q_raw = q_raw + fetch(q_raw, c=1)
    q_mean, q_pieces = kernel_call(
        mean_body, 1, [inverse, *around([q_raw] * 4, "x")], [None] * 5,
        [f32(RANK, columns), bf16(6 * RANK, columns)], [None] * 2,
    )

    out = error_calls(gathered, hidden, basis, q_pieces, error)
    return out[None], q_mean.T


def solution(mesh):
    placed = (
        P("dp", "tensor"),
        P(("dp", "tensor"), None),
        P("dp", None, "tensor"),
        P("tensor", None),
    )
    return jax.shard_map(
        on_device,
        mesh=mesh,
        in_specs=placed,
        out_specs=(P("dp", None, "tensor"), P("tensor", None)),
        check_vma=False,
    )
```

```python
import jax
import jax.numpy as jnp
from jax import lax
from jax.experimental import pallas as pl
from jax.experimental.pallas import tpu as pltpu
from jax.sharding import PartitionSpec as P

AXES = ("dp", "tensor")
RANK = 32
NX, NC, NZ, NY = 4, 2, 4, 4
N_DP = NX * NC
TOK = 128
BLOCK = 512
F32, BF16 = jnp.float32, jnp.bfloat16
SMEM = pl.BlockSpec(memory_space=pltpu.SMEM)


def receive_from(x=0, c=0, z=0, y=0):
    pairs = []
    for ix in range(NX):
        for ic in range(NC):
            for iz in range(NZ):
                for iy in range(NY):
                    target = ((ix * NC + ic) * NZ + iz) * NY + iy
                    source = (((ix + x) % NX * NC + (ic + c) % NC) * NZ + (iz + z) % NZ) * NY + (iy + y) % NY
                    pairs.append((source, target))
    return pairs


def fetch(array, **offsets):
    return lax.ppermute(array, AXES, receive_from(**offsets))


def around(arrays, axis):
    return [arrays[0]] + [fetch(arrays[k], **{axis: k}) for k in (1, 2, 3)]


def f32(*shape):
    return jax.ShapeDtypeStruct(shape, F32)


def bf16(*shape):
    return jax.ShapeDtypeStruct(shape, BF16)


def whole(array):
    zeros = (0,) * len(array.shape)
    return pl.BlockSpec(tuple(array.shape), lambda *_: zeros)


def kernel_call(body, grid, operands, in_specs, outs, out_specs, scratch=(), aliases=None, vmem_mib=16, after=()):
    count = len(operands)
    operands = [*operands, *after]
    in_specs = [*in_specs, *[pl.BlockSpec(memory_space=pltpu.HBM)] * len(after)]

    def call(*refs):
        body(*refs[:count], *refs[count + len(after):])

    return pl.pallas_call(
        call,
        grid=(grid,),
        in_specs=[whole(a) if s is None else s for a, s in zip(operands, in_specs)],
        out_specs=[whole(a) if s is None else s for a, s in zip(outs, out_specs)],
        out_shape=outs,
        scratch_shapes=list(scratch),
        input_output_aliases=aliases or {},
        compiler_params=pltpu.CompilerParams(vmem_limit_bytes=vmem_mib * 2 ** 20),
        cost_estimate=pl.CostEstimate(flops=2 ** 20, bytes_accessed=2 ** 16, transcendentals=0),
    )(*operands)


def split3(value):
    high = value.astype(BF16)
    rest = value - high.astype(F32)
    middle = rest.astype(BF16)
    low = (rest - middle.astype(F32)).astype(BF16)
    return jnp.concatenate([high, middle, low], axis=0)


def fold3(product):
    return product[:RANK] + (product[RANK:2 * RANK] + product[2 * RANK:])


def dot_nt(a, b):
    return lax.dot_general(a, b, (((1,), (1,)), ((), ())), preferred_element_type=F32)


def dot_nn(a, b):
    return jnp.dot(a, b, preferred_element_type=F32)


def hq_body(q_t, h, out, pieces):
    @pl.when(pl.program_id(0) == 0)
    def _():
        pieces[...] = split3(q_t[...])

    part = fold3(dot_nt(pieces[...], h[...]))
    for y in range(NY):
        out[y] = part[:, y * TOK:(y + 1) * TOK]


def eq_body(q_t, e, out, pieces):
    @pl.when(pl.program_id(0) == 0)
    def _():
        pieces[...] = split3(q_t[...])

    out[...] = fold3(dot_nt(pieces[...], e[...]))


def power_body(hq, c, eq, out, lhs):
    @pl.when(pl.program_id(0) == 0)
    def _():
        total = hq[0]
        for t in range(1, NZ * NY):
            total += hq[t]
        lhs[...] = split3(total)

    term = fold3(dot_nn(lhs[...], c[...])) + eq[...]
    for j in range(out.shape[0]):
        out[j] = term[:, j * BLOCK:(j + 1) * BLOCK]


def sum_body(*refs):
    total = refs[0][...]
    for ref in refs[1:-1]:
        total += ref[...]
    refs[-1][...] = total


def sum_copies_body(*refs):
    total = (refs[0][...] + refs[1][...]) + (refs[2][...] + refs[3][...])
    refs[4][...] = jnp.broadcast_to(total[None], refs[4].shape)


def sum_pieces_body(pieces, out):
    total = pieces[0]
    for r in range(1, N_DP):
        total += pieces[r]
    out[...] = total


def cp_body(power_pieces, c, power, pieces, out, acc):
    i = pl.program_id(0)

    @pl.when(i == 0)
    def _():
        acc[...] = jnp.zeros_like(acc)

    block = jnp.concatenate([power_pieces[j] for j in range(power_pieces.shape[0])], axis=1)
    power[...] = block
    split = split3(block)
    pieces[...] = split
    acc[...] += fold3(dot_nt(split, c[...]))

    @pl.when(i == pl.num_programs(0) - 1)
    def _():
        out[...] = jnp.broadcast_to(acc[...][None], out.shape)


def basis_body(power, pieces, e, ep, inverse, basis, acc, gram):
    i = pl.program_id(0)

    @pl.when(i == 0)
    def _():
        acc[...] = jnp.zeros_like(acc)
        gram[...] = lax.dot_general(
            power[...], power[...], (((1,), (1,)), ((), ())), precision=lax.Precision.HIGHEST, preferred_element_type=F32
        )

    acc[...] += fold3(dot_nn(pieces[...], e[...]))

    @pl.when(i == pl.num_programs(0) - 1)
    def _():
        ep[...] = acc[...]
        row = lax.broadcasted_iota(jnp.int32, (RANK, 2 * RANK), 0)
        column = lax.broadcasted_iota(jnp.int32, (RANK, 2 * RANK), 1)
        work = jnp.concatenate([gram[...], jnp.zeros((RANK, RANK), F32)], axis=1)
        work = jnp.where(column == row + RANK, 1.0, work)
        for j in range(RANK):
            factor = work[:, j:j + 1] / work[j:j + 1, j:j + 1]
            work = work - jnp.where(row > j, factor, 0.0) * work[j:j + 1, :]
        pivots = jnp.sum(jnp.where(column == row, work, 0.0), axis=1, keepdims=True)
        inv = work[:, RANK:] / jnp.sqrt(pivots)
        inverse[...] = inv
        b = jnp.dot(inv, power[...], precision=lax.Precision.HIGHEST, preferred_element_type=F32)
        b = split3(b)
        high, middle, low = b[:RANK], b[RANK:2 * RANK], b[2 * RANK:]
        basis[...] = jnp.concatenate([high, high, middle, high, low, middle], axis=0)


def q_body(cp, h, ep, out, acc):
    i = pl.program_id(0)

    @pl.when(i == 0)
    def _():
        acc[...] = ep[...]

    left = split3(jnp.concatenate([cp[y] for y in range(NY)], axis=1))
    acc[...] += fold3(dot_nn(left, h[...]))

    @pl.when(i == NZ - 1)
    def _():
        out[...] = acc[...]


def mean_body(inverse, p0, p1, p2, p3, q_mean, pieces):
    total = (p0[...] + p1[...]) + (p2[...] + p3[...])
    mean = jnp.dot(inverse[...], total, precision=lax.Precision.HIGHEST, preferred_element_type=F32) * (1.0 / N_DP)
    q_mean[...] = mean
    s = split3(mean)
    high, middle, low = s[:RANK], s[RANK:2 * RANK], s[2 * RANK:]
    pieces[...] = jnp.concatenate([high, middle, high, low, high, middle], axis=0)


def rest_body(basis, q, e, out):
    update = lax.dot_general(basis[...], q[...], (((0,), (0,)), ((), ())), preferred_element_type=F32)
    out[...] = e[...].astype(F32) - update


def turn_body(h, out):
    out[...] = h[...].T


def error_body(c, h_t, rest, out):
    gradient = dot_nn(h_t[...], c[...])
    out[...] = (gradient.T + rest[...]).astype(BF16)


def error_calls(gathered, h_t, basis, q, e):
    rows, columns = e.shape
    wide = 2 * BLOCK
    in_rows = pl.BlockSpec((wide, columns), lambda i: (i, 0))
    (rest,) = kernel_call(
        rest_body, rows // wide, [basis, q, e],
        [pl.BlockSpec((basis.shape[0], wide), lambda i: (0, i)), None, in_rows], [f32(rows, columns)], [in_rows], vmem_mib=56,
    )
    return kernel_call(
        error_body, rows // wide, [gathered, h_t, rest],
        [pl.BlockSpec((gathered.shape[0], wide), lambda i: (0, i)), None, in_rows],
        [bf16(rows, columns)], [in_rows], vmem_mib=56,
    )[0]


def on_device(hidden, cotangent, error, q_start):
    error = error[0]
    rows = cotangent.shape[1]
    columns = hidden.shape[1]
    n_blocks = rows // BLOCK

    gathered = lax.all_gather(cotangent, "tensor", axis=0, tiled=True)

    q_t = q_start.T
    (hq,) = kernel_call(
        hq_body, NZ, [q_t, hidden], [None, pl.BlockSpec((4 * TOK, columns), lambda i: (i, 0))],
        [f32(NZ * NY, RANK, TOK)], [pl.BlockSpec((NY, RANK, TOK), lambda i: (i, 0, 0))],
        scratch=[pltpu.VMEM((3 * RANK, columns), BF16)],
    )
    hq = lax.all_to_all(hq, "tensor", 0, 0)
    row_spec = pl.BlockSpec((BLOCK, columns), lambda i: (i, 0))
    column_spec = pl.BlockSpec((RANK, BLOCK), lambda i: (0, i))
    (eq,) = kernel_call(
        eq_body, n_blocks, [q_t, error], [None, row_spec], [f32(RANK, rows)], [column_spec],
        scratch=[pltpu.VMEM((3 * RANK, columns), BF16)],
    )
    stack_specs = [
        pl.BlockSpec((BLOCK, 4 * TOK), lambda i, n=n: (jnp.clip(i - 2 * n, 0, 1), 0)) for n in range(4)
    ]
    wide = n_blocks // 2
    c_spec = pl.BlockSpec((TOK, wide * BLOCK), lambda i: (0, i))
    wide_spec = pl.BlockSpec((RANK, wide * BLOCK), lambda i: (0, i))
    piece_spec = pl.BlockSpec((wide, RANK, BLOCK), lambda i: (i, 0, 0))
    (terms,) = kernel_call(
        power_body, 2, [hq, cotangent, eq], [None, c_spec, wide_spec], [f32(N_DP, RANK, BLOCK)], [piece_spec],
        scratch=[pltpu.VMEM((3 * RANK, TOK), BF16)],
    )
    terms = lax.all_to_all(terms, "dp", 0, 0)
    (hidden_t,) = kernel_call(
        turn_body, NZ, [hidden], [pl.BlockSpec((4 * TOK, columns), lambda i: (i, 0))], [bf16(columns, hidden.shape[0])],
        [pl.BlockSpec((columns, 4 * TOK), lambda i: (0, i))], vmem_mib=56, after=[eq],
    )
    (piece,) = kernel_call(sum_pieces_body, 1, [terms], [None], [f32(RANK, BLOCK)], [None], after=[hidden_t])
    (piece,) = kernel_call(sum_body, 1, around([piece] * 4, "y"), [None] * 4, [f32(RANK, BLOCK)], [None])
    (copies,) = kernel_call(
        sum_copies_body, 1, around([piece] * 4, "z"), [None] * 4, [f32(N_DP, RANK, BLOCK)], [None],
    )
    power_pieces = lax.all_to_all(copies, "dp", 0, 0)
    power, pieces, cp = kernel_call(
        cp_body, 2, [power_pieces, cotangent], [piece_spec, c_spec],
        [f32(RANK, rows), bf16(3 * RANK, rows), f32(NZ * NY, RANK, TOK)],
        [wide_spec, pl.BlockSpec((3 * RANK, wide * BLOCK), lambda i: (0, i)), None],
        scratch=[pltpu.VMEM((RANK, TOK), F32)],
    )
    cp = lax.all_to_all(cp, "tensor", 0, 0)
    ep, inverse, basis = kernel_call(
        basis_body, n_blocks, [power, pieces, error],
        [None, pl.BlockSpec((3 * RANK, BLOCK), lambda i: (0, i)), row_spec],
        [f32(RANK, columns), f32(RANK, RANK), bf16(6 * RANK, rows)], [None] * 3,
        scratch=[pltpu.VMEM((RANK, columns), F32), pltpu.VMEM((RANK, RANK), F32)],
    )
    (q_raw,) = kernel_call(
        q_body, NZ, [cp, hidden, ep],
        [pl.BlockSpec((NY, RANK, TOK), lambda i: (i, 0, 0)), pl.BlockSpec((4 * TOK, columns), lambda i: (i, 0)), None],
        [f32(RANK, columns)], [None], scratch=[pltpu.VMEM((RANK, columns), F32)],
    )
    q_raw = q_raw + fetch(q_raw, c=1)
    q_mean, q_pieces = kernel_call(
        mean_body, 1, [inverse, *around([q_raw] * 4, "x")], [None] * 5,
        [f32(RANK, columns), bf16(6 * RANK, columns)], [None] * 2,
    )

    out = error_calls(gathered, hidden_t, basis, q_pieces, error)
    return out[None], q_mean.T


def solution(mesh):
    placed = (
        P("dp", "tensor"),
        P(("dp", "tensor"), None),
        P("dp", None, "tensor"),
        P("tensor", None),
    )
    return jax.shard_map(
        on_device,
        mesh=mesh,
        in_specs=placed,
        out_specs=(P("dp", None, "tensor"), P("tensor", None)),
        check_vma=False,
    )
```

```python
import jax
import jax.numpy as jnp
from jax import lax
from jax.experimental import pallas as pl
from jax.experimental.pallas import tpu as pltpu
from jax.sharding import PartitionSpec as P

AXES = ("dp", "tensor")
RANK = 32
NX, NC, NZ, NY = 4, 2, 4, 4
N_DP = NX * NC
TOK = 128
BLOCK = 512
F32, BF16 = jnp.float32, jnp.bfloat16
SMEM = pl.BlockSpec(memory_space=pltpu.SMEM)


def receive_from(x=0, c=0, z=0, y=0):
    pairs = []
    for ix in range(NX):
        for ic in range(NC):
            for iz in range(NZ):
                for iy in range(NY):
                    target = ((ix * NC + ic) * NZ + iz) * NY + iy
                    source = (((ix + x) % NX * NC + (ic + c) % NC) * NZ + (iz + z) % NZ) * NY + (iy + y) % NY
                    pairs.append((source, target))
    return pairs


def fetch(array, **offsets):
    return lax.ppermute(array, AXES, receive_from(**offsets))


def around(arrays, axis):
    return [arrays[0]] + [fetch(arrays[k], **{axis: k}) for k in (1, 2, 3)]


def f32(*shape):
    return jax.ShapeDtypeStruct(shape, F32)


def bf16(*shape):
    return jax.ShapeDtypeStruct(shape, BF16)


def whole(array):
    zeros = (0,) * len(array.shape)
    return pl.BlockSpec(tuple(array.shape), lambda *_: zeros)


def kernel_call(body, grid, operands, in_specs, outs, out_specs, scratch=(), aliases=None, vmem_mib=16, after=()):
    count = len(operands)
    operands = [*operands, *after]
    in_specs = [*in_specs, *[pl.BlockSpec(memory_space=pltpu.HBM)] * len(after)]

    def call(*refs):
        body(*refs[:count], *refs[count + len(after):])

    return pl.pallas_call(
        call,
        grid=(grid,),
        in_specs=[whole(a) if s is None else s for a, s in zip(operands, in_specs)],
        out_specs=[whole(a) if s is None else s for a, s in zip(outs, out_specs)],
        out_shape=outs,
        scratch_shapes=list(scratch),
        input_output_aliases=aliases or {},
        compiler_params=pltpu.CompilerParams(vmem_limit_bytes=vmem_mib * 2 ** 20),
        cost_estimate=pl.CostEstimate(flops=2 ** 20, bytes_accessed=2 ** 16, transcendentals=0),
    )(*operands)


def split3(value):
    high = value.astype(BF16)
    rest = value - high.astype(F32)
    middle = rest.astype(BF16)
    low = (rest - middle.astype(F32)).astype(BF16)
    return jnp.concatenate([high, middle, low], axis=0)


def fold3(product):
    return product[:RANK] + (product[RANK:2 * RANK] + product[2 * RANK:])


def dot_nt(a, b):
    return lax.dot_general(a, b, (((1,), (1,)), ((), ())), preferred_element_type=F32)


def dot_nn(a, b):
    return jnp.dot(a, b, preferred_element_type=F32)


def hq_body(q_t, h, out, pieces):
    @pl.when(pl.program_id(0) == 0)
    def _():
        pieces[...] = split3(q_t[...])

    part = fold3(dot_nt(pieces[...], h[...]))
    for y in range(NY):
        out[y] = part[:, y * TOK:(y + 1) * TOK]


def eq_body(q_t, e, out, pieces):
    @pl.when(pl.program_id(0) == 0)
    def _():
        pieces[...] = split3(q_t[...])

    out[...] = fold3(dot_nt(pieces[...], e[...]))


def power_body(hq, c, eq, out, lhs):
    @pl.when(pl.program_id(0) == 0)
    def _():
        total = hq[0]
        for t in range(1, NZ * NY):
            total += hq[t]
        lhs[...] = split3(total)

    term = fold3(dot_nn(lhs[...], c[...])) + eq[...]
    for j in range(out.shape[0]):
        out[j] = term[:, j * BLOCK:(j + 1) * BLOCK]


def sum_body(*refs):
    total = refs[0][...]
    for ref in refs[1:-1]:
        total += ref[...]
    refs[-1][...] = total


def place_copies_body(pos, *refs):
    out = refs[4]
    for k in range(4):
        out[:, (pos[0] + k) % 4] = jnp.broadcast_to(refs[k][...][None], (N_DP, RANK, TOK))


def sum_pieces_body(pos, pieces, *outs):
    total = pieces[0]
    for r in range(1, N_DP):
        total += pieces[r]
    quarters = outs[4]
    for k in range(4):
        quarters[k] = total[:, k * TOK:(k + 1) * TOK]
    for k in range(4):
        outs[k][...] = quarters[(pos[0] + 4 - k) % 4]


def cp_body(power_pieces, c, power, pieces, out, acc):
    i = pl.program_id(0)

    @pl.when(i == 0)
    def _():
        acc[...] = jnp.zeros_like(acc)

    block = jnp.concatenate(
        [power_pieces[j, k] for j in range(power_pieces.shape[0]) for k in range(4)], axis=1
    )
    power[...] = block
    split = split3(block)
    pieces[...] = split
    acc[...] += fold3(dot_nt(split, c[...]))

    @pl.when(i == pl.num_programs(0) - 1)
    def _():
        out[...] = jnp.broadcast_to(acc[...][None], out.shape)


def basis_body(power, pieces, e, ep, inverse, basis, acc, gram):
    i = pl.program_id(0)

    @pl.when(i == 0)
    def _():
        acc[...] = jnp.zeros_like(acc)
        gram[...] = lax.dot_general(
            power[...], power[...], (((1,), (1,)), ((), ())), precision=lax.Precision.HIGHEST, preferred_element_type=F32
        )

    acc[...] += fold3(dot_nn(pieces[...], e[...]))

    @pl.when(i == pl.num_programs(0) - 1)
    def _():
        ep[...] = acc[...]
        row = lax.broadcasted_iota(jnp.int32, (RANK, 2 * RANK), 0)
        column = lax.broadcasted_iota(jnp.int32, (RANK, 2 * RANK), 1)
        work = jnp.concatenate([gram[...], jnp.zeros((RANK, RANK), F32)], axis=1)
        work = jnp.where(column == row + RANK, 1.0, work)
        for j in range(RANK):
            factor = work[:, j:j + 1] / work[j:j + 1, j:j + 1]
            work = work - jnp.where(row > j, factor, 0.0) * work[j:j + 1, :]
        pivots = jnp.sum(jnp.where(column == row, work, 0.0), axis=1, keepdims=True)
        inv = work[:, RANK:] / jnp.sqrt(pivots)
        inverse[...] = inv
        b = jnp.dot(inv, power[...], precision=lax.Precision.HIGHEST, preferred_element_type=F32)
        b = split3(b)
        high, middle, low = b[:RANK], b[RANK:2 * RANK], b[2 * RANK:]
        basis[...] = jnp.concatenate([high, high, middle, high, low, middle], axis=0)


def q_body(cp, h, ep, out, acc):
    i = pl.program_id(0)

    @pl.when(i == 0)
    def _():
        acc[...] = ep[...]

    left = split3(jnp.concatenate([cp[y] for y in range(NY)], axis=1))
    acc[...] += fold3(dot_nn(left, h[...]))

    @pl.when(i == NZ - 1)
    def _():
        out[...] = acc[...]


def mean_body(inverse, p0, p1, p2, p3, q_mean, pieces):
    total = (p0[...] + p1[...]) + (p2[...] + p3[...])
    mean = jnp.dot(inverse[...], total, precision=lax.Precision.HIGHEST, preferred_element_type=F32) * (1.0 / N_DP)
    q_mean[...] = mean
    s = split3(mean)
    high, middle, low = s[:RANK], s[RANK:2 * RANK], s[2 * RANK:]
    pieces[...] = jnp.concatenate([high, middle, high, low, high, middle], axis=0)


def rest_body(basis, q, e, out):
    update = lax.dot_general(basis[...], q[...], (((0,), (0,)), ((), ())), preferred_element_type=F32)
    out[...] = e[...].astype(F32) - update


def error_body(c, h, rest, out):
    gradient = lax.dot_general(c[...], h[...], (((0,), (0,)), ((), ())), preferred_element_type=F32)
    out[...] = (gradient + rest[...]).astype(BF16)


def error_calls(gathered, h, basis, q, e):
    rows, columns = e.shape
    wide = 2 * BLOCK
    in_rows = pl.BlockSpec((wide, columns), lambda i: (i, 0))
    (rest,) = kernel_call(
        rest_body, rows // wide, [basis, q, e],
        [pl.BlockSpec((basis.shape[0], wide), lambda i: (0, i)), None, in_rows], [f32(rows, columns)], [in_rows], vmem_mib=56,
    )
    in_rows = pl.BlockSpec((BLOCK, columns), lambda i: (i, 0))
    return kernel_call(
        error_body, rows // BLOCK, [gathered, h, rest],
        [pl.BlockSpec((gathered.shape[0], BLOCK), lambda i: (0, i)), None, in_rows],
        [bf16(rows, columns)], [in_rows], vmem_mib=56,
    )[0]


def on_device(hidden, cotangent, error, q_start):
    error = error[0]
    rows = cotangent.shape[1]
    columns = hidden.shape[1]
    n_blocks = rows // BLOCK

    gathered = lax.all_gather(cotangent, "tensor", axis=0, tiled=True)

    q_t = q_start.T
    (hq,) = kernel_call(
        hq_body, NZ, [q_t, hidden], [None, pl.BlockSpec((4 * TOK, columns), lambda i: (i, 0))],
        [f32(NZ * NY, RANK, TOK)], [pl.BlockSpec((NY, RANK, TOK), lambda i: (i, 0, 0))],
        scratch=[pltpu.VMEM((3 * RANK, columns), BF16)],
    )
    hq = lax.all_to_all(hq, "tensor", 0, 0)
    row_spec = pl.BlockSpec((BLOCK, columns), lambda i: (i, 0))
    column_spec = pl.BlockSpec((RANK, BLOCK), lambda i: (0, i))
    (eq,) = kernel_call(
        eq_body, n_blocks, [q_t, error], [None, row_spec], [f32(RANK, rows)], [column_spec],
        scratch=[pltpu.VMEM((3 * RANK, columns), BF16)],
    )
    stack_specs = [
        pl.BlockSpec((BLOCK, 4 * TOK), lambda i, n=n: (jnp.clip(i - 2 * n, 0, 1), 0)) for n in range(4)
    ]
    wide = n_blocks // 2
    c_spec = pl.BlockSpec((TOK, wide * BLOCK), lambda i: (0, i))
    wide_spec = pl.BlockSpec((RANK, wide * BLOCK), lambda i: (0, i))
    piece_spec = pl.BlockSpec((wide, RANK, BLOCK), lambda i: (i, 0, 0))
    (terms,) = kernel_call(
        power_body, 2, [hq, cotangent, eq], [None, c_spec, wide_spec], [f32(N_DP, RANK, BLOCK)], [piece_spec],
        scratch=[pltpu.VMEM((3 * RANK, TOK), BF16)],
    )
    terms = lax.all_to_all(terms, "dp", 0, 0)
    pos = jnp.reshape(lax.axis_index("tensor") % NY, (1,)).astype(jnp.int32)
    quarter = f32(RANK, TOK)
    sends = kernel_call(
        sum_pieces_body, 1, [pos, terms], [SMEM, None], [quarter] * 4, [None] * 4,
        scratch=[pltpu.VMEM((4, RANK, TOK), F32)],
    )
    (piece,) = kernel_call(sum_body, 1, around(sends, "y"), [None] * 4, [quarter], [None])
    (piece,) = kernel_call(sum_body, 1, around([piece] * 4, "z"), [None] * 4, [quarter], [None])
    (copies,) = kernel_call(
        place_copies_body, 1, [pos, *around([piece] * 4, "y")], [SMEM] + [None] * 4, [f32(N_DP, 4, RANK, TOK)], [None],
    )
    power_pieces = lax.all_to_all(copies, "dp", 0, 0)
    power, pieces, cp = kernel_call(
        cp_body, 2, [power_pieces, cotangent],
        [pl.BlockSpec((wide, 4, RANK, TOK), lambda i: (i, 0, 0, 0)), c_spec],
        [f32(RANK, rows), bf16(3 * RANK, rows), f32(NZ * NY, RANK, TOK)],
        [wide_spec, pl.BlockSpec((3 * RANK, wide * BLOCK), lambda i: (0, i)), None],
        scratch=[pltpu.VMEM((RANK, TOK), F32)],
    )
    cp = lax.all_to_all(cp, "tensor", 0, 0)
    ep, inverse, basis = kernel_call(
        basis_body, n_blocks, [power, pieces, error],
        [None, pl.BlockSpec((3 * RANK, BLOCK), lambda i: (0, i)), row_spec],
        [f32(RANK, columns), f32(RANK, RANK), bf16(6 * RANK, rows)], [None] * 3,
        scratch=[pltpu.VMEM((RANK, columns), F32), pltpu.VMEM((RANK, RANK), F32)],
    )
    (q_raw,) = kernel_call(
        q_body, NZ, [cp, hidden, ep],
        [pl.BlockSpec((NY, RANK, TOK), lambda i: (i, 0, 0)), pl.BlockSpec((4 * TOK, columns), lambda i: (i, 0)), None],
        [f32(RANK, columns)], [None], scratch=[pltpu.VMEM((RANK, columns), F32)],
    )
    q_raw = q_raw + fetch(q_raw, c=1)
    q_mean, q_pieces = kernel_call(
        mean_body, 1, [inverse, *around([q_raw] * 4, "x")], [None] * 5,
        [f32(RANK, columns), bf16(6 * RANK, columns)], [None] * 2,
    )

    out = error_calls(gathered, hidden, basis, q_pieces, error)
    return out[None], q_mean.T


def solution(mesh):
    placed = (
        P("dp", "tensor"),
        P(("dp", "tensor"), None),
        P("dp", None, "tensor"),
        P("tensor", None),
    )
    return jax.shard_map(
        on_device,
        mesh=mesh,
        in_specs=placed,
        out_specs=(P("dp", None, "tensor"), P("tensor", None)),
        check_vma=False,
    )
```

```python
import jax
import jax.numpy as jnp
from jax import lax
from jax.experimental import pallas as pl
from jax.experimental.pallas import tpu as pltpu
from jax.sharding import PartitionSpec as P

AXES = ("dp", "tensor")
RANK = 32
NX, NC, NZ, NY = 4, 2, 4, 4
N_DP = NX * NC
TOK = 128
BLOCK = 512
F32, BF16 = jnp.float32, jnp.bfloat16
SMEM = pl.BlockSpec(memory_space=pltpu.SMEM)


def receive_from(x=0, c=0, z=0, y=0):
    pairs = []
    for ix in range(NX):
        for ic in range(NC):
            for iz in range(NZ):
                for iy in range(NY):
                    target = ((ix * NC + ic) * NZ + iz) * NY + iy
                    source = (((ix + x) % NX * NC + (ic + c) % NC) * NZ + (iz + z) % NZ) * NY + (iy + y) % NY
                    pairs.append((source, target))
    return pairs


def fetch(array, **offsets):
    return lax.ppermute(array, AXES, receive_from(**offsets))


def around(arrays, axis):
    return [arrays[0]] + [fetch(arrays[k], **{axis: k}) for k in (1, 2, 3)]


def f32(*shape):
    return jax.ShapeDtypeStruct(shape, F32)


def bf16(*shape):
    return jax.ShapeDtypeStruct(shape, BF16)


def whole(array):
    zeros = (0,) * len(array.shape)
    return pl.BlockSpec(tuple(array.shape), lambda *_: zeros)


def kernel_call(body, grid, operands, in_specs, outs, out_specs, scratch=(), aliases=None, vmem_mib=16, after=()):
    count = len(operands)
    operands = [*operands, *after]
    in_specs = [*in_specs, *[pl.BlockSpec(memory_space=pltpu.HBM)] * len(after)]

    def call(*refs):
        body(*refs[:count], *refs[count + len(after):])

    return pl.pallas_call(
        call,
        grid=(grid,),
        in_specs=[whole(a) if s is None else s for a, s in zip(operands, in_specs)],
        out_specs=[whole(a) if s is None else s for a, s in zip(outs, out_specs)],
        out_shape=outs,
        scratch_shapes=list(scratch),
        input_output_aliases=aliases or {},
        compiler_params=pltpu.CompilerParams(vmem_limit_bytes=vmem_mib * 2 ** 20),
        cost_estimate=pl.CostEstimate(flops=2 ** 20, bytes_accessed=2 ** 16, transcendentals=0),
    )(*operands)


def split3(value):
    high = value.astype(BF16)
    rest = value - high.astype(F32)
    middle = rest.astype(BF16)
    low = (rest - middle.astype(F32)).astype(BF16)
    return jnp.concatenate([high, middle, low], axis=0)


def fold3(product):
    return product[:RANK] + (product[RANK:2 * RANK] + product[2 * RANK:])


def dot_nt(a, b):
    return lax.dot_general(a, b, (((1,), (1,)), ((), ())), preferred_element_type=F32)


def dot_nn(a, b):
    return jnp.dot(a, b, preferred_element_type=F32)


def hq_body(q_t, h, out, pieces):
    @pl.when(pl.program_id(0) == 0)
    def _():
        pieces[...] = split3(q_t[...])

    part = fold3(dot_nt(pieces[...], h[...]))
    for y in range(NY):
        out[y] = part[:, y * TOK:(y + 1) * TOK]


def eq_body(q_t, e, out, pieces):
    @pl.when(pl.program_id(0) == 0)
    def _():
        pieces[...] = split3(q_t[...])

    out[...] = fold3(dot_nt(pieces[...], e[...]))


def power_body(hq, c, eq, out, lhs):
    @pl.when(pl.program_id(0) == 0)
    def _():
        total = hq[0]
        for t in range(1, NZ * NY):
            total += hq[t]
        lhs[...] = split3(total)

    term = fold3(dot_nn(lhs[...], c[...])) + eq[...]
    for j in range(out.shape[0]):
        out[j] = term[:, j * BLOCK:(j + 1) * BLOCK]


def sum_body(*refs):
    total = refs[0][...]
    for ref in refs[1:-1]:
        total += ref[...]
    refs[-1][...] = total


def place_copies_body(pos, *refs):
    out = refs[4]
    for k in range(4):
        out[:, (pos[0] + k) % 4] = jnp.broadcast_to(refs[k][...][None], (N_DP, RANK, TOK))


def sum_pieces_body(pos, pieces, *outs):
    total = pieces[0]
    for r in range(1, N_DP):
        total += pieces[r]
    quarters = outs[4]
    for k in range(4):
        quarters[k] = total[:, k * TOK:(k + 1) * TOK]
    for k in range(4):
        outs[k][...] = quarters[(pos[0] + 4 - k) % 4]


def cp_body(power_pieces, c, power, pieces, out, acc):
    i = pl.program_id(0)

    @pl.when(i == 0)
    def _():
        acc[...] = jnp.zeros_like(acc)

    block = jnp.concatenate(
        [power_pieces[j, k] for j in range(power_pieces.shape[0]) for k in range(4)], axis=1
    )
    power[...] = block
    split = split3(block)
    pieces[...] = split
    acc[...] += fold3(dot_nt(split, c[...]))

    @pl.when(i == pl.num_programs(0) - 1)
    def _():
        out[...] = jnp.broadcast_to(acc[...][None], out.shape)


def basis_body(power, pieces, e, ep, inverse, basis, acc, gram):
    i = pl.program_id(0)

    @pl.when(i == 0)
    def _():
        acc[...] = jnp.zeros_like(acc)
        gram[...] = lax.dot_general(
            power[...], power[...], (((1,), (1,)), ((), ())), precision=lax.Precision.HIGHEST, preferred_element_type=F32
        )

    acc[...] += fold3(dot_nn(pieces[...], e[...]))

    @pl.when(i == pl.num_programs(0) - 1)
    def _():
        ep[...] = acc[...]
        row = lax.broadcasted_iota(jnp.int32, (RANK, 2 * RANK), 0)
        column = lax.broadcasted_iota(jnp.int32, (RANK, 2 * RANK), 1)
        work = jnp.concatenate([gram[...], jnp.zeros((RANK, RANK), F32)], axis=1)
        work = jnp.where(column == row + RANK, 1.0, work)
        for j in range(RANK):
            factor = work[:, j:j + 1] / work[j:j + 1, j:j + 1]
            work = work - jnp.where(row > j, factor, 0.0) * work[j:j + 1, :]
        pivots = jnp.sum(jnp.where(column == row, work, 0.0), axis=1, keepdims=True)
        inv = work[:, RANK:] / jnp.sqrt(pivots)
        inverse[...] = inv
        b = jnp.dot(inv, power[...], precision=lax.Precision.HIGHEST, preferred_element_type=F32)
        b = split3(b)
        high, middle, low = b[:RANK], b[RANK:2 * RANK], b[2 * RANK:]
        basis[...] = jnp.concatenate([high, high, middle, high, low, middle], axis=0)


def q_body(cp, h, ep, out, acc):
    i = pl.program_id(0)

    @pl.when(i == 0)
    def _():
        acc[...] = ep[...]

    left = split3(jnp.concatenate([cp[y] for y in range(NY)], axis=1))
    acc[...] += fold3(dot_nn(left, h[...]))

    @pl.when(i == NZ - 1)
    def _():
        out[...] = acc[...]


def mean_body(inverse, p0, p1, p2, p3, q_mean, pieces):
    total = (p0[...] + p1[...]) + (p2[...] + p3[...])
    mean = jnp.dot(inverse[...], total, precision=lax.Precision.HIGHEST, preferred_element_type=F32) * (1.0 / N_DP)
    q_mean[...] = mean
    s = split3(mean)
    high, middle, low = s[:RANK], s[RANK:2 * RANK], s[2 * RANK:]
    pieces[...] = jnp.concatenate([high, middle, high, low, high, middle], axis=0)


def rest_body(basis, q, e, out):
    update = lax.dot_general(basis[...], q[...], (((0,), (0,)), ((), ())), preferred_element_type=F32)
    out[...] = e[...].astype(F32) - update


def turn_body(h, out):
    out[...] = h[...].T


def error_body(c, h_t, rest, out):
    gradient = dot_nn(h_t[...], c[...])
    out[...] = (gradient.T + rest[...]).astype(BF16)


def error_calls(gathered, h_t, basis, q, e):
    rows, columns = e.shape
    wide = 2 * BLOCK
    in_rows = pl.BlockSpec((wide, columns), lambda i: (i, 0))
    (rest,) = kernel_call(
        rest_body, rows // wide, [basis, q, e],
        [pl.BlockSpec((basis.shape[0], wide), lambda i: (0, i)), None, in_rows], [f32(rows, columns)], [in_rows], vmem_mib=56,
    )
    return kernel_call(
        error_body, rows // wide, [gathered, h_t, rest],
        [pl.BlockSpec((gathered.shape[0], wide), lambda i: (0, i)), None, in_rows],
        [bf16(rows, columns)], [in_rows], vmem_mib=56,
    )[0]


def on_device(hidden, cotangent, error, q_start):
    error = error[0]
    rows = cotangent.shape[1]
    columns = hidden.shape[1]
    n_blocks = rows // BLOCK

    gathered = lax.all_gather(cotangent, "tensor", axis=0, tiled=True)

    q_t = q_start.T
    (hq,) = kernel_call(
        hq_body, NZ, [q_t, hidden], [None, pl.BlockSpec((4 * TOK, columns), lambda i: (i, 0))],
        [f32(NZ * NY, RANK, TOK)], [pl.BlockSpec((NY, RANK, TOK), lambda i: (i, 0, 0))],
        scratch=[pltpu.VMEM((3 * RANK, columns), BF16)],
    )
    hq = lax.all_to_all(hq, "tensor", 0, 0)
    row_spec = pl.BlockSpec((BLOCK, columns), lambda i: (i, 0))
    column_spec = pl.BlockSpec((RANK, BLOCK), lambda i: (0, i))
    (eq,) = kernel_call(
        eq_body, n_blocks, [q_t, error], [None, row_spec], [f32(RANK, rows)], [column_spec],
        scratch=[pltpu.VMEM((3 * RANK, columns), BF16)],
    )
    stack_specs = [
        pl.BlockSpec((BLOCK, 4 * TOK), lambda i, n=n: (jnp.clip(i - 2 * n, 0, 1), 0)) for n in range(4)
    ]
    wide = n_blocks // 2
    c_spec = pl.BlockSpec((TOK, wide * BLOCK), lambda i: (0, i))
    wide_spec = pl.BlockSpec((RANK, wide * BLOCK), lambda i: (0, i))
    piece_spec = pl.BlockSpec((wide, RANK, BLOCK), lambda i: (i, 0, 0))
    (terms,) = kernel_call(
        power_body, 2, [hq, cotangent, eq], [None, c_spec, wide_spec], [f32(N_DP, RANK, BLOCK)], [piece_spec],
        scratch=[pltpu.VMEM((3 * RANK, TOK), BF16)],
    )
    terms = lax.all_to_all(terms, "dp", 0, 0)
    pos = jnp.reshape(lax.axis_index("tensor") % NY, (1,)).astype(jnp.int32)
    quarter = f32(RANK, TOK)
    sends = kernel_call(
        sum_pieces_body, 1, [pos, terms], [SMEM, None], [quarter] * 4, [None] * 4,
        scratch=[pltpu.VMEM((4, RANK, TOK), F32)],
    )
    (piece,) = kernel_call(sum_body, 1, around(sends, "y"), [None] * 4, [quarter], [None])
    (piece,) = kernel_call(sum_body, 1, around([piece] * 4, "z"), [None] * 4, [quarter], [None])
    (copies,) = kernel_call(
        place_copies_body, 1, [pos, *around([piece] * 4, "y")], [SMEM] + [None] * 4, [f32(N_DP, 4, RANK, TOK)], [None],
    )
    (hidden_t,) = kernel_call(
        turn_body, NZ, [hidden], [pl.BlockSpec((4 * TOK, columns), lambda i: (i, 0))], [bf16(columns, hidden.shape[0])],
        [pl.BlockSpec((columns, 4 * TOK), lambda i: (0, i))], vmem_mib=56, after=[copies],
    )
    power_pieces = lax.all_to_all(copies, "dp", 0, 0)
    power, pieces, cp = kernel_call(
        cp_body, 2, [power_pieces, cotangent],
        [pl.BlockSpec((wide, 4, RANK, TOK), lambda i: (i, 0, 0, 0)), c_spec],
        [f32(RANK, rows), bf16(3 * RANK, rows), f32(NZ * NY, RANK, TOK)],
        [wide_spec, pl.BlockSpec((3 * RANK, wide * BLOCK), lambda i: (0, i)), None],
        scratch=[pltpu.VMEM((RANK, TOK), F32)], after=[hidden_t],
    )
    cp = lax.all_to_all(cp, "tensor", 0, 0)
    ep, inverse, basis = kernel_call(
        basis_body, n_blocks, [power, pieces, error],
        [None, pl.BlockSpec((3 * RANK, BLOCK), lambda i: (0, i)), row_spec],
        [f32(RANK, columns), f32(RANK, RANK), bf16(6 * RANK, rows)], [None] * 3,
        scratch=[pltpu.VMEM((RANK, columns), F32), pltpu.VMEM((RANK, RANK), F32)],
    )
    (q_raw,) = kernel_call(
        q_body, NZ, [cp, hidden, ep],
        [pl.BlockSpec((NY, RANK, TOK), lambda i: (i, 0, 0)), pl.BlockSpec((4 * TOK, columns), lambda i: (i, 0)), None],
        [f32(RANK, columns)], [None], scratch=[pltpu.VMEM((RANK, columns), F32)],
    )
    q_raw = q_raw + fetch(q_raw, c=1)
    q_mean, q_pieces = kernel_call(
        mean_body, 1, [inverse, *around([q_raw] * 4, "x")], [None] * 5,
        [f32(RANK, columns), bf16(6 * RANK, columns)], [None] * 2,
    )

    out = error_calls(gathered, hidden_t, basis, q_pieces, error)
    return out[None], q_mean.T


def solution(mesh):
    placed = (
        P("dp", "tensor"),
        P(("dp", "tensor"), None),
        P("dp", None, "tensor"),
        P("tensor", None),
    )
    return jax.shard_map(
        on_device,
        mesh=mesh,
        in_specs=placed,
        out_specs=(P("dp", None, "tensor"), P("tensor", None)),
        check_vma=False,
    )
```
